32 devices in a mesh: grp: 2 (over y), row: 4 (over z), col: 2 (over x), rep: 2 (over core).
Axes of the slice: x: 2, y: 2, z: 4, core: 2. Of those that a mesh axis runs over, the one named last changes fastest.
Arguments:
- f_rta: float32 [3, 8, 20480], P(None, None, ('grp', 'row', 'col', 'rep')), parts along dimension 2, may hold values from -6 to 6
- relax_time: float32 [8, 20480], P(None, ('grp', 'row', 'col', 'rep')), parts along dimension 1, may hold values from 0.15 to 1.2
- scatter_tiles: bfloat16 [4096, 128, 128], P(('grp', 'row', 'col', 'rep')), parts along dimension 0, may hold values from -0.109375 to 0.109375
- tile_row: int32 [4096], P(('grp', 'row', 'col', 'rep')), parts along dimension 0, may hold values from 0 to 19
- tile_col: int32 [4096], P(('grp', 'row', 'col', 'rep')), parts along dimension 0, may hold values from 0 to 79, as said below
Outputs:
- f_out: float32 [3, 8, 20480], P(None, None, ('grp', 'row', 'col', 'rep')), parts along dimension 2
The draws below stay inside these ranges and needn't reach their ends.
There are 2 independent parts, one for each index of `grp`. The reference program is written for one: setup_inputs(seed, part) draws one part's arguments, and reference() takes and returns one part's arrays. A program takes and returns all parts, laid end to end along the dimension named above; each array names one. Nothing has to cross between parts.
Inputs may be any that keep to these rules, and one draw needn't show every extreme that they name: `tile_col`: A tile held by the device at col index c has a column block b owned by that col index: (b // 10) % 2 == c. Block b lives on the device at row index b // 20, col index (b // 10) % 2, rep index (b // 5) % 2. Tiles may repeat a block pair; their terms add.
All inputs are finite; a program needn't handle non-finite values.
Results may differ from the reference program's by a relative error of at most 0.0021.
Values may be sent and summed in bfloat16 or wider, within the bound.
A program may use at most 64 MiB of HBM per device.

```python
import math
import jax
import jax.numpy as jnp
from jax import lax

DIRS = 3
TEMPS = 8
TILE = 128
BLK_DEV = 5
TILES_DEV = 128
ITERS = 2
STATES = 10240
TILES = 2048
N_ROW = 4
N_COL = 2
N_REP = 2


def draw_tile_col(key, part):
    key = jax.random.fold_in(key, 11)
    devices = N_ROW * N_COL * N_REP
    group_size = BLK_DEV * N_REP
    candidates = group_size * N_ROW
    candidate = jax.random.randint(key, (devices, TILES_DEV), 0, candidates)
    position = jnp.arange(TILES_DEV, dtype=jnp.int32)[None, :]
    candidate = jnp.where(position == 0, 0, candidate)
    candidate = jnp.where(position == TILES_DEV - 1, candidates - 1, candidate)
    col_index = jnp.arange(devices, dtype=jnp.int32) // N_REP % N_COL
    block = candidate // group_size * (group_size * N_COL) + col_index[:, None] * group_size + candidate % group_size
    return block.reshape(devices * TILES_DEV).astype(jnp.int32)


def with_ends(drawn, stream_key, least, high):
    spot = [jax.random.randint(jax.random.fold_in(stream_key, axis), (), 0, length) for axis, length in enumerate(drawn.shape)]
    longest = drawn.shape.index(max(drawn.shape))
    neighbour = spot[:longest] + [(spot[longest] + 1) % drawn.shape[longest]] + spot[longest + 1:]
    return drawn.at[tuple(spot)].set(least).at[tuple(neighbour)].set(high)


def block_scale(key, shape, cuts, low, largest):
    level, own = 1.0, jax.random.fold_in(key, 6)
    for dim, shards_of in cuts:
        heights = jnp.exp(jax.random.uniform(jax.random.fold_in(own, dim), (shards_of,), jnp.float32, low / len(cuts), largest / len(cuts)))
        level = level * jnp.repeat(heights, shape[dim] // shards_of).reshape([-1 if axis == dim else 1 for axis in range(len(shape))])
    return level


def scatter_about(own_key, shape, width, limit, split=(), kind=jnp.bfloat16):
    values = jax.random.normal(own_key, shape, jnp.float32) * width
    if len(split) > 0:
        values = block_scale(own_key, shape, split, -0.22, 0.18) * values
    return jnp.clip(values, min=-limit, max=limit).astype(kind)


def setup_inputs(seed: int = 0, part: int = 0) -> dict:
    splits = jax.random.split(jax.random.key(seed), 6)
    part_splits = jax.random.split(jax.random.fold_in(splits[5], part), 6)
    return {
        "f_rta": scatter_about(part_splits[0], (DIRS, TEMPS, STATES), 1.0, 6.0, ((2, 16),), jnp.float32),
        "relax_time": jnp.clip(jnp.exp(math.log(1.2) - 2.0794415 * jax.random.uniform(part_splits[1], (TEMPS, STATES), jnp.float32) ** block_scale(part_splits[1], (TEMPS, STATES), ((1, 16),), -0.2, 0.2)), 0.15, 1.2),
        "scatter_tiles": scatter_about(part_splits[2], (TILES, TILE, TILE), (TILE * TILES_DEV // BLK_DEV) ** -0.5, 0.109375, ((0, 16),)),
        "tile_row": with_ends(jax.random.randint(part_splits[3], (TILES,), 0, BLK_DEV * N_COL * N_REP), jax.random.fold_in(part_splits[3], 1), 0, (BLK_DEV * N_COL * N_REP) - 1).astype(jnp.int32),
        "tile_col": draw_tile_col(jax.random.fold_in(jax.random.fold_in(splits[5], part), 71), part),
    }


def reference(f_rta, relax_time, scatter_tiles, tile_row, tile_col):
    components = DIRS * TEMPS
    devices = N_ROW * N_COL * N_REP
    group_rows = BLK_DEV * N_COL * N_REP
    block_count = BLK_DEV * devices
    tile_sets = scatter_tiles.reshape(devices, TILES_DEV, TILE, TILE)
    row_sets = tile_row.reshape(devices, TILES_DEV)
    col_sets = tile_col.reshape(devices, TILES_DEV)
    owner_rows = (jnp.arange(devices, dtype=jnp.int32) // (N_COL * N_REP)).astype(jnp.int32)
    local_rows = jnp.arange(group_rows, dtype=jnp.int32)
    current = f_rta
    for sweep in range(ITERS):
        vector_bf = current.astype(jnp.bfloat16).reshape(components, block_count, TILE)

        def add_device(accumulated, device_items):
            block_tiles, tile_rows, tile_cols, owner_row = device_items
            picked = jnp.take(vector_bf, tile_cols, axis=1)
            products = jnp.einsum("krc,dkc->kdr", block_tiles.astype(jnp.float32), picked.astype(jnp.float32))
            onehot = (local_rows[:, None] == tile_rows[None, :]).astype(jnp.float32)
            block_sums = jnp.einsum("gk,kdr->dgr", onehot, products, precision=lax.Precision.HIGHEST)
            row_start = (owner_row * group_rows).astype(jnp.int32)
            anchor = jnp.zeros((), jnp.int32)
            previous = lax.dynamic_slice(accumulated, (anchor, row_start, anchor), (components, group_rows, TILE))
            return lax.dynamic_update_slice(accumulated, previous + block_sums, (anchor, row_start, anchor)), None

        initial = jnp.zeros((components, block_count, TILE), jnp.float32)
        accumulated, _ = lax.scan(add_device, initial, (tile_sets, row_sets, col_sets, owner_rows))
        current = f_rta + relax_time[None] * accumulated.reshape(DIRS, TEMPS, block_count * TILE)
    return current
```

```python
import functools

import jax
import jax.numpy as jnp
from jax import lax
from jax.experimental import pallas as pl
from jax.experimental.pallas import tpu as pltpu
from jax.sharding import PartitionSpec as P

DIRS = 3
TEMPS = 8
COMP = DIRS * TEMPS
TILE = 128
BLK_DEV = 5
ITERS = 2
UNROLL = 16
CHUNKS = 4
ROWS = BLK_DEV * COMP
PAD = 128
MESH = pl.DeviceIdType.MESH


def kernel(sizes, f_ref, relax_ref, row_ref, col_ref, tiles_hbm, out_ref,
           tiles, vsend, slab, vec, chain, part, recv, table_v, table,
           tile_sem, table_sem, vs_send, vs_recv, fw_send, fw_recv, p_send, p_recv):
    n_row, n_col, n_rep, n_tiles = sizes
    grp, row = lax.axis_index("grp"), lax.axis_index("row")
    col, rep = lax.axis_index("col"), lax.axis_index("rep")
    per = n_tiles // CHUNKS

    row_peers = list(range(1, n_row))
    sum_peers = [(dc, dr) for dc in range(n_col) for dr in range(n_rep) if (dc, dr) != (0, 0)]
    rep_peers = list(range(1, n_rep))

    def at_row(step):
        return (grp, lax.rem(row + step, n_row), col, rep)

    def at_sum(dc, dr):
        return (grp, row, lax.rem(col + dc, n_col), lax.rem(rep + dr, n_rep))

    barrier = pltpu.get_barrier_semaphore()
    for step in row_peers:
        pl.semaphore_signal(barrier, inc=1, device_id=at_row(step), device_id_type=MESH)
    for dc, dr in sum_peers:
        pl.semaphore_signal(barrier, inc=1, device_id=at_sum(dc, dr), device_id_type=MESH)

    loads = []
    for i in range(CHUNKS):
        load = pltpu.make_async_copy(tiles_hbm.at[pl.ds(i * per, per)], tiles.at[pl.ds(i * per, per)], tile_sem.at[i])
        load.start()
        loads.append(load)

    def pack(it, source):
        blocks = [source[:, b * TILE:(b + 1) * TILE] for b in range(BLK_DEV)]
        blocks.append(jnp.zeros((PAD - ROWS, TILE), jnp.float32))
        vsend[it] = jnp.concatenate(blocks, axis=0).astype(jnp.bfloat16)

    pack(0, f_ref[...])
    pl.semaphore_wait(barrier, len(row_peers) + len(sum_peers))

    def gather_start(it):
        own = row * n_rep + rep
        sends = []
        for step in row_peers:
            copy = pltpu.make_async_remote_copy(
                src_ref=vsend.at[it], dst_ref=slab.at[it, own],
                send_sem=vs_send.at[it, step], recv_sem=vs_recv.at[it, step],
                device_id=at_row(step), device_id_type=MESH)
            copy.start()
            sends.append(copy)
        for step in rep_peers:
            copy = pltpu.make_async_remote_copy(
                src_ref=vsend.at[it], dst_ref=slab.at[it, own],
                send_sem=fw_send.at[it, 0, step], recv_sem=fw_recv.at[it, 0, step],
                device_id=at_sum(0, step), device_id_type=MESH)
            copy.start()
            sends.append(copy)
        return sends

    def unpack(it, index, value):
        vec[pl.ds(index * BLK_DEV, BLK_DEV)] = (
            value.astype(jnp.float32)[:ROWS].reshape(BLK_DEV, COMP, TILE))

    def gather_finish(it, sends):
        unpack(it, row * n_rep + rep, vsend[it])
        forwards = []
        for step in row_peers:
            origin = lax.rem(row + n_row - step, n_row)
            slot = origin * n_rep + rep
            pltpu.make_async_remote_copy(
                src_ref=vsend.at[it], dst_ref=slab.at[it, slot],
                send_sem=vs_send.at[it, step], recv_sem=vs_recv.at[it, step],
                device_id=at_row(step), device_id_type=MESH).wait_recv()
            for other in rep_peers:
                copy = pltpu.make_async_remote_copy(
                    src_ref=slab.at[it, slot], dst_ref=slab.at[it, slot],
                    send_sem=fw_send.at[it, step, other], recv_sem=fw_recv.at[it, step, other],
                    device_id=at_sum(0, other), device_id_type=MESH)
                copy.start()
                forwards.append(copy)
            unpack(it, slot, slab[it, slot])
        for step in [0] + row_peers:
            origin = lax.rem(row + n_row - step, n_row)
            for other in rep_peers:
                slot = origin * n_rep + lax.rem(rep + n_rep - other, n_rep)
                pltpu.make_async_remote_copy(
                    src_ref=vsend.at[it], dst_ref=slab.at[it, slot],
                    send_sem=fw_send.at[it, step, other], recv_sem=fw_recv.at[it, step, other],
                    device_id=at_sum(0, other), device_id_type=MESH).wait_recv()
                unpack(it, slot, slab[it, slot])
        return sends + forwards

    pending = gather_start(0)

    rows_lane = jnp.broadcast_to(row_ref[...], (n_tiles, n_tiles))
    rows_sub = rows_lane.T
    sub = lax.broadcasted_iota(jnp.int32, (n_tiles, n_tiles), 0)
    lane = lax.broadcasted_iota(jnp.int32, (n_tiles, n_tiles), 1)
    before = (rows_sub == rows_lane) & (sub < lane)
    previous = jnp.max(jnp.where(before, sub + 1, 0), axis=0, keepdims=True)
    last = jnp.max(jnp.where(rows_sub == lane, sub + 1, 0), axis=0, keepdims=True)
    group_size = BLK_DEV * n_rep
    span = group_size * n_col
    magic = -(-65536 // span)
    assert (magic * span - 65536) * span * n_row < 65536
    columns = col_ref[...]
    quotient = (columns * magic) >> 16
    rest = columns - quotient * span
    for _ in range(n_col - 1):
        rest = jnp.where(rest >= group_size, rest - group_size, rest)
    block = quotient * group_size + rest
    table_v[0:1, :] = previous
    table_v[1:2, :] = last
    table_v[2:3, :] = block
    table_copy = pltpu.make_async_copy(table_v, table, table_sem)
    table_copy.start()
    chain[0] = jnp.zeros((COMP, TILE), jnp.float32)
    table_copy.wait()

    def multiply(first, count):
        def body(i, carry):
            base = first + i * UNROLL
            products = []
            for u in range(UNROLL):
                picked = vec[table[2, base + u]].astype(jnp.bfloat16)
                products.append(lax.dot_general(
                    picked, tiles[base + u], (((1,), (1,)), ((), ())),
                    preferred_element_type=jnp.float32))
            for u in range(UNROLL):
                chain[base + u + 1] = chain[table[0, base + u]] + products[u]
            return carry
        lax.fori_loop(0, count // UNROLL, body, 0)

    for it in range(ITERS):
        pending = gather_finish(it, pending)
        if it == 0:
            for i in range(CHUNKS):
                loads[i].wait()
                multiply(i * per, per)
        else:
            multiply(0, n_tiles)

        for dc, dr in reversed(sum_peers):
            owner = lax.rem(col + dc, n_col) * n_rep + lax.rem(rep + dr, n_rep)
            index = dc * n_rep + dr
            for b in range(BLK_DEV):
                part[it, index, b] = chain[table[1, owner * BLK_DEV + b]]
            copy = pltpu.make_async_remote_copy(
                src_ref=part.at[it, index], dst_ref=recv.at[it, index],
                send_sem=p_send.at[it, index], recv_sem=p_recv.at[it, index],
                device_id=at_sum(dc, dr), device_id_type=MESH)
            copy.start()
            pending.append(copy)
        owner = col * n_rep + rep
        sums = [chain[table[1, owner * BLK_DEV + b]] for b in range(BLK_DEV)]
        for dc, dr in sum_peers:
            index = dc * n_rep + dr
            pltpu.make_async_remote_copy(
                src_ref=part.at[it, index], dst_ref=recv.at[it, index],
                send_sem=p_send.at[it, index], recv_sem=p_recv.at[it, index],
                device_id=at_sum(dc, dr), device_id_type=MESH).wait_recv()
            sums = [sums[b] + recv[it, index, b] for b in range(BLK_DEV)]
        summed = jnp.concatenate(sums, axis=1)
        relax = jnp.concatenate([relax_ref[...]] * DIRS, axis=0)
        current = f_ref[...] + relax * summed
        if it + 1 < ITERS:
            pack(it + 1, current)
            pending = pending + gather_start(it + 1)
        else:
            out_ref[...] = current
    for copy in pending:
        copy.wait_send()


def shards(sizes, f_rta, relax_time, scatter_tiles, tile_row, tile_col):
    n_row, n_col, n_rep, n_tiles = sizes
    width = f_rta.shape[-1]
    members, slots = n_col * n_rep, n_row * n_rep
    dma = pltpu.SemaphoreType.DMA
    vmem = pl.BlockSpec(memory_space=pltpu.VMEM)
    out = pl.pallas_call(
        functools.partial(kernel, sizes),
        out_shape=jax.ShapeDtypeStruct((COMP, width), jnp.float32),
        in_specs=[vmem, vmem, vmem, vmem, pl.BlockSpec(memory_space=pl.ANY)],
        out_specs=vmem,
        scratch_shapes=[
            pltpu.VMEM((n_tiles, TILE, TILE), jnp.bfloat16),
            pltpu.VMEM((ITERS, PAD, TILE), jnp.bfloat16),
            pltpu.VMEM((ITERS, slots, PAD, TILE), jnp.bfloat16),
            pltpu.VMEM((slots * BLK_DEV, COMP, TILE), jnp.float32),
            pltpu.VMEM((n_tiles + 1, COMP, TILE), jnp.float32),
            pltpu.VMEM((ITERS, members, BLK_DEV, COMP, TILE), jnp.float32),
            pltpu.VMEM((ITERS, members, BLK_DEV, COMP, TILE), jnp.float32),
            pltpu.VMEM((8, n_tiles), jnp.int32),
            pltpu.SMEM((8, n_tiles), jnp.int32),
            dma((CHUNKS,)),
            dma,
            dma((ITERS, n_row)),
            dma((ITERS, n_row)),
            dma((ITERS, n_row, n_rep)),
            dma((ITERS, n_row, n_rep)),
            dma((ITERS, members)),
            dma((ITERS, members)),
        ],
        compiler_params=pltpu.CompilerParams(
            collective_id=0, has_side_effects=True, vmem_limit_bytes=40 * 2**20),
    )(
        f_rta.reshape(COMP, width),
        relax_time,
        tile_row.reshape(1, n_tiles),
        tile_col.reshape(1, n_tiles),
        scatter_tiles,
    )
    return out.reshape(DIRS, TEMPS, width)


def solution(mesh):
    in_specs = (
        P(None, None, ("grp", "row", "col", "rep")),
        P(None, ("grp", "row", "col", "rep")),
        P(("grp", "row", "col", "rep"), None, None),
        P(("grp", "row", "col", "rep")),
        P(("grp", "row", "col", "rep")),
    )
    out_specs = P(None, None, ("grp", "row", "col", "rep"))

    def whole(f_rta, relax_time, scatter_tiles, tile_row, tile_col):
        n_tiles = tile_row.shape[0] // mesh.size
        sizes = (mesh.shape["row"], mesh.shape["col"], mesh.shape["rep"], n_tiles)
        return jax.shard_map(
            functools.partial(shards, sizes), mesh=mesh, in_specs=in_specs,
            out_specs=out_specs, check_vma=False,
        )(f_rta, relax_time, scatter_tiles, tile_row, tile_col)

    return whole
```

```python
import functools

import jax
import jax.numpy as jnp
from jax import lax
from jax.experimental import pallas as pl
from jax.experimental.pallas import tpu as pltpu
from jax.sharding import PartitionSpec as P

DIRS = 3
TEMPS = 8
COMP = DIRS * TEMPS
TILE = 128
BLK_DEV = 5
ITERS = 2
CHUNKS = 4
ROWS = BLK_DEV * COMP
PAD = 128
MESH = pl.DeviceIdType.MESH


def kernel(sizes, f_hbm, relax_hbm, row_hbm, col_hbm, tiles_hbm, out_ref,
           f_ref, relax_ref, row_ref, col_ref, tiles, turned, vsend, slab, vec, chain, part, recv, table_v, table,
           tile_sem, in_sem, table_sem, vs_send, vs_recv, fw_send, fw_recv, p_send, p_recv):
    n_row, n_col, n_rep, n_tiles = sizes
    grp, row = lax.axis_index("grp"), lax.axis_index("row")
    col, rep = lax.axis_index("col"), lax.axis_index("rep")
    per = n_tiles // CHUNKS

    row_peers = list(range(1, n_row))
    sum_peers = [(dc, dr) for dc in range(n_col) for dr in range(n_rep) if (dc, dr) != (0, 0)]
    rep_peers = list(range(1, n_rep))

    wait_order = sorted(row_peers, key=lambda step: (min(step, n_row - step), step))

    def at_row(step):
        return (grp, lax.rem(row + step, n_row), col, rep)

    def at_sum(dc, dr):
        return (grp, row, lax.rem(col + dc, n_col), lax.rem(rep + dr, n_rep))

    barrier = pltpu.get_barrier_semaphore()
    for step in row_peers:
        pl.semaphore_signal(barrier, inc=1, device_id=at_row(step), device_id_type=MESH)
    for dc, dr in sum_peers:
        pl.semaphore_signal(barrier, inc=1, device_id=at_sum(dc, dr), device_id_type=MESH)

    small = []
    for i, (source, target) in enumerate(
            [(f_hbm, f_ref), (row_hbm, row_ref), (col_hbm, col_ref), (relax_hbm, relax_ref)]):
        load = pltpu.make_async_copy(source, target, in_sem.at[i])
        load.start()
        small.append(load)
    loads = []
    for i in range(CHUNKS):
        load = pltpu.make_async_copy(tiles_hbm.at[pl.ds(i * per, per)], tiles.at[pl.ds(i * per, per)], tile_sem.at[i])
        load.start()
        loads.append(load)

    def pack(it, source):
        blocks = [source[:, b * TILE:(b + 1) * TILE] for b in range(BLK_DEV)]
        blocks.append(jnp.zeros((PAD - ROWS, TILE), jnp.float32))
        vsend[it] = jnp.concatenate(blocks, axis=0).astype(jnp.bfloat16)

    small[0].wait()
    pack(0, f_ref[...])
    pl.semaphore_wait(barrier, len(row_peers) + len(sum_peers))

    def gather_start(it):
        own = row * n_rep + rep
        sends = []
        for step in wait_order:
            copy = pltpu.make_async_remote_copy(
                src_ref=vsend.at[it], dst_ref=slab.at[it, own],
                send_sem=vs_send.at[it, step], recv_sem=vs_recv.at[it, step],
                device_id=at_row(step), device_id_type=MESH)
            copy.start()
            sends.append(copy)
        for step in rep_peers:
            copy = pltpu.make_async_remote_copy(
                src_ref=vsend.at[it], dst_ref=slab.at[it, own],
                send_sem=fw_send.at[it, 0, step], recv_sem=fw_recv.at[it, 0, step],
                device_id=at_sum(0, step), device_id_type=MESH)
            copy.start()
            sends.append(copy)
        return sends

    def unpack(it, index, value):
        vec[pl.ds(index * BLK_DEV, BLK_DEV)] = (
            value.astype(jnp.float32)[:ROWS].reshape(BLK_DEV, COMP, TILE))

    def gather_finish(it, sends):
        unpack(it, row * n_rep + rep, vsend[it])
        forwards = []
        for step in wait_order:
            origin = lax.rem(row + n_row - step, n_row)
            slot = origin * n_rep + rep
            pltpu.make_async_remote_copy(
                src_ref=vsend.at[it], dst_ref=slab.at[it, slot],
                send_sem=vs_send.at[it, step], recv_sem=vs_recv.at[it, step],
                device_id=at_row(step), device_id_type=MESH).wait_recv()
            for other in rep_peers:
                copy = pltpu.make_async_remote_copy(
                    src_ref=slab.at[it, slot], dst_ref=slab.at[it, slot],
                    send_sem=fw_send.at[it, step, other], recv_sem=fw_recv.at[it, step, other],
                    device_id=at_sum(0, other), device_id_type=MESH)
                copy.start()
                forwards.append(copy)
        for step in wait_order:
            slot = lax.rem(row + n_row - step, n_row) * n_rep + rep
            unpack(it, slot, slab[it, slot])
        for step in [0] + wait_order:
            origin = lax.rem(row + n_row - step, n_row)
            for other in rep_peers:
                slot = origin * n_rep + lax.rem(rep + n_rep - other, n_rep)
                pltpu.make_async_remote_copy(
                    src_ref=vsend.at[it], dst_ref=slab.at[it, slot],
                    send_sem=fw_send.at[it, step, other], recv_sem=fw_recv.at[it, step, other],
                    device_id=at_sum(0, other), device_id_type=MESH).wait_recv()
                unpack(it, slot, slab[it, slot])
        return sends + forwards

    pending = gather_start(0)

    for load in small[1:]:
        load.wait()
    rows_lane = jnp.broadcast_to(row_ref[...], (n_tiles, n_tiles))
    rows_sub = rows_lane.T
    sub = lax.broadcasted_iota(jnp.int32, (n_tiles, n_tiles), 0)
    lane = lax.broadcasted_iota(jnp.int32, (n_tiles, n_tiles), 1)
    before = (rows_sub == rows_lane) & (sub < lane)
    previous = jnp.max(jnp.where(before, sub + 1, 0), axis=0, keepdims=True)
    last = jnp.max(jnp.where(rows_sub == lane, sub + 1, 0), axis=0, keepdims=True)
    group_size = BLK_DEV * n_rep
    span = group_size * n_col
    magic = -(-65536 // span)
    assert (magic * span - 65536) * span * n_row < 65536
    columns = col_ref[...]
    quotient = (columns * magic) >> 16
    rest = columns - quotient * span
    for _ in range(n_col - 1):
        rest = jnp.where(rest >= group_size, rest - group_size, rest)
    block = quotient * group_size + rest
    table_v[0:1, :] = previous
    table_v[1:2, :] = last
    table_v[2:3, :] = block
    table_copy = pltpu.make_async_copy(table_v, table, table_sem)
    table_copy.start()
    chain[0] = jnp.zeros((COMP, TILE), jnp.float32)
    for i in range(CHUNKS):
        loads[i].wait()
        for k in range(i * per, (i + 1) * per):
            turned[k] = tiles[k].T
    table_copy.wait()

    def multiply():
        for k in range(n_tiles):
            picked = vec[table[2, k]].astype(jnp.bfloat16)
            product = jnp.dot(picked, turned[k], preferred_element_type=jnp.float32)
            chain[k + 1] = chain[table[0, k]] + product

    for it in range(ITERS):
        pending = gather_finish(it, pending)
        multiply()

        for dc, dr in reversed(sum_peers):
            owner = lax.rem(col + dc, n_col) * n_rep + lax.rem(rep + dr, n_rep)
            index = dc * n_rep + dr
            for b in range(BLK_DEV):
                part[it, index, b] = chain[table[1, owner * BLK_DEV + b]]
            copy = pltpu.make_async_remote_copy(
                src_ref=part.at[it, index], dst_ref=recv.at[it, index],
                send_sem=p_send.at[it, index], recv_sem=p_recv.at[it, index],
                device_id=at_sum(dc, dr), device_id_type=MESH)
            copy.start()
            pending.append(copy)
        owner = col * n_rep + rep
        sums = [chain[table[1, owner * BLK_DEV + b]] for b in range(BLK_DEV)]
        for dc, dr in sum_peers:
            index = dc * n_rep + dr
            pltpu.make_async_remote_copy(
                src_ref=part.at[it, index], dst_ref=recv.at[it, index],
                send_sem=p_send.at[it, index], recv_sem=p_recv.at[it, index],
                device_id=at_sum(dc, dr), device_id_type=MESH).wait_recv()
            sums = [sums[b] + recv[it, index, b] for b in range(BLK_DEV)]
        summed = jnp.concatenate(sums, axis=1)
        relax = jnp.concatenate([relax_ref[...]] * DIRS, axis=0)
        current = f_ref[...] + relax * summed
        if it + 1 < ITERS:
            pack(it + 1, current)
            pending = pending + gather_start(it + 1)
        else:
            out_ref[...] = current
    for copy in pending:
        copy.wait_send()


def shards(sizes, f_rta, relax_time, scatter_tiles, tile_row, tile_col):
    n_row, n_col, n_rep, n_tiles = sizes
    width = f_rta.shape[-1]
    members, slots = n_col * n_rep, n_row * n_rep
    dma = pltpu.SemaphoreType.DMA
    vmem = pl.BlockSpec(memory_space=pltpu.VMEM)
    out = pl.pallas_call(
        functools.partial(kernel, sizes),
        out_shape=jax.ShapeDtypeStruct((COMP, width), jnp.float32),
        in_specs=[pl.BlockSpec(memory_space=pltpu.HBM)] * 5,
        out_specs=vmem,
        scratch_shapes=[
            pltpu.VMEM((COMP, width), jnp.float32),
            pltpu.VMEM((TEMPS, width), jnp.float32),
            pltpu.VMEM((1, n_tiles), jnp.int32),
            pltpu.VMEM((1, n_tiles), jnp.int32),
            pltpu.VMEM((n_tiles, TILE, TILE), jnp.bfloat16),
            pltpu.VMEM((n_tiles, TILE, TILE), jnp.bfloat16),
            pltpu.VMEM((ITERS, PAD, TILE), jnp.bfloat16),
            pltpu.VMEM((ITERS, slots, PAD, TILE), jnp.bfloat16),
            pltpu.VMEM((slots * BLK_DEV, COMP, TILE), jnp.float32),
            pltpu.VMEM((n_tiles + 1, COMP, TILE), jnp.float32),
            pltpu.VMEM((ITERS, members, BLK_DEV, COMP, TILE), jnp.float32),
            pltpu.VMEM((ITERS, members, BLK_DEV, COMP, TILE), jnp.float32),
            pltpu.VMEM((8, n_tiles), jnp.int32),
            pltpu.SMEM((8, n_tiles), jnp.int32),
            dma((CHUNKS,)),
            dma((4,)),
            dma,
            dma((ITERS, n_row)),
            dma((ITERS, n_row)),
            dma((ITERS, n_row, n_rep)),
            dma((ITERS, n_row, n_rep)),
            dma((ITERS, members)),
            dma((ITERS, members)),
        ],
        compiler_params=pltpu.CompilerParams(
            collective_id=0, has_side_effects=True, vmem_limit_bytes=56 * 2**20),
    )(
        f_rta.reshape(COMP, width),
        relax_time,
        tile_row.reshape(1, n_tiles),
        tile_col.reshape(1, n_tiles),
        scatter_tiles,
    )
    return out.reshape(DIRS, TEMPS, width)


def solution(mesh):
    in_specs = (
        P(None, None, ("grp", "row", "col", "rep")),
        P(None, ("grp", "row", "col", "rep")),
        P(("grp", "row", "col", "rep"), None, None),
        P(("grp", "row", "col", "rep")),
        P(("grp", "row", "col", "rep")),
    )
    out_specs = P(None, None, ("grp", "row", "col", "rep"))

    def whole(f_rta, relax_time, scatter_tiles, tile_row, tile_col):
        n_tiles = tile_row.shape[0] // mesh.size
        sizes = (mesh.shape["row"], mesh.shape["col"], mesh.shape["rep"], n_tiles)
        return jax.shard_map(
            functools.partial(shards, sizes), mesh=mesh, in_specs=in_specs,
            out_specs=out_specs, check_vma=False,
        )(f_rta, relax_time, scatter_tiles, tile_row, tile_col)

    return whole
```
